32 devices in a mesh: dp: 4 (over y, x), blk: 8 (over z, core).
Axes of the slice: x: 2, y: 2, z: 4, core: 2. Of those that a mesh axis runs over, the one named last changes fastest.
Arguments:
- queries: bfloat16 [8192, 1664], P(('dp', 'blk')), parts along dimension 0, as said below
- keys: bfloat16 [8192, 1664], P(('dp', 'blk')), parts along dimension 0, as said below
- values: bfloat16 [8192, 1664], P(('dp', 'blk')), parts along dimension 0, may hold values from -6 to 6
- residual_in: bfloat16 [8192, 1664], P(('dp', 'blk')), parts along dimension 0, as said below
- out_proj: bfloat16 [1664, 1664], replicated, may hold values from -0.15625 to 0.15625
- ln_gain: float32 [1664], replicated, may hold values from 0.1 to 1.9
- merge_proj: bfloat16 [6656, 4096], P('blk'), as said below
- out_gain: float32 [4096], replicated, may hold values from 0.1 to 1.9
- image_rows: int32 [16], P('dp'), parts along dimension 0, may hold values from 1 to 192, 512 in all
- owners: int32 [2048, 1], P(('dp', 'blk')), parts along dimension 0, may hold values from 0 to 7; in each aligned block of 64 rows (0 to 63, 64 to 127, ...) at most 16 rows name the same one
Outputs:
- delivered: bfloat16 [4096, 4096], P(('dp', 'blk')), parts along dimension 0
The draws below stay inside these ranges and needn't reach their ends.
There are 4 independent parts, one for each index of `dp`. The reference program is written for one: setup_inputs(seed, part) draws one part's arguments, and reference() takes and returns one part's arrays. A program takes and returns all parts, laid end to end along the dimension named above; an argument that names none is the same for every part. Nothing has to cross between parts.
Inputs may be any that keep to these rules, and one draw needn't show every extreme that they name: `image_rows`: images lie end to end; their merged rows sum to 512, and one image has exactly the most. `owners`: among the merged rows of one block no owner is named more than 16 times. `queries`: Real-valued; no structure is promised. `keys`: Real-valued; no structure is promised. `residual_in`: Real-valued; no structure is promised. `merge_proj`: Real-valued; no structure is promised.
All inputs are finite; a program needn't handle non-finite values.
Results may differ from the reference program's by a relative error of at most 0.017.
Values may be sent and summed in bfloat16 or wider, within the bound.
A program may use at most 128 MiB of HBM per device.

```python
import math
import jax
import jax.numpy as jnp
import numpy as np
from jax import lax

D = 1664
HEADS = 16
HDIM = 104
OUTW = 4096
TOK_DEV = 256
TOKENS = 2048
MERGED = 6656
MROWS = 512
MROW_DEV = 64
FEAT_DEV = 832
NIMG = 4
REACH = 3
CAP = 16
N_BLK = 8


def direction():
    place = jnp.arange(D, dtype=jnp.int32)
    return (1 - 2 * ((place * place + 3 * place) // 7 % 2)).astype(jnp.float32)


def query_base(key):
    return jax.random.normal(jax.random.fold_in(key, 1), (TOKENS, D), jnp.float32)


def far_partners(key):
    base = query_base(key)
    place = jnp.arange(TOKENS, dtype=jnp.int32)
    offset = REACH * TOK_DEV - 1 - jax.random.randint(jax.random.fold_in(key, 3), (TOKENS,), 0, TOK_DEV // 2)
    target = ((place + offset) % TOKENS).astype(jnp.int32)
    planted = jax.random.randint(jax.random.fold_in(key, 4), (TOKENS,), 0, 4) != 0
    strength = jax.random.uniform(jax.random.fold_in(key, 5), (TOKENS,), jnp.float32, 0.7, 1.2) * (8.0 / HDIM ** 0.5)
    factor = jnp.where(planted, strength, 0.0)
    return factor[:, None] * base[target]


def draw_queries(key, part):
    drawn = query_base(key)
    return jnp.clip(drawn, -24.0, 24.0).astype(jnp.bfloat16)


def draw_keys(key, part):
    drawn = jax.random.normal(jax.random.fold_in(key, 2), (TOKENS, D), jnp.float32) + far_partners(key)
    return jnp.clip(drawn, -24.0, 24.0).astype(jnp.bfloat16)


def draw_residual_in(key, part):
    blocks = TOKENS // TOK_DEV
    noise = jnp.clip(jax.random.normal(jax.random.fold_in(key, 21), (TOKENS, D), jnp.float32), -6.0, 6.0)
    block_strength = jax.random.uniform(jax.random.fold_in(key, 22), (blocks,), jnp.float32, 0.0, 0.6)
    row_sign = jnp.where(jax.random.randint(jax.random.fold_in(key, 23), (TOKENS // 4,), 0, 2) == 0, 1.0, -1.0)
    row_size = jax.random.uniform(jax.random.fold_in(key, 24), (TOKENS // 4,), jnp.float32, 0.5, 1.5)
    place = jnp.arange(TOKENS, dtype=jnp.int32)
    along = block_strength[place // TOK_DEV] * row_sign[place // 4] * row_size[place // 4]
    stream = 0.25 * noise + along[:, None] * direction()[None, :]
    return jnp.clip(stream, -2.5, 2.5).astype(jnp.bfloat16)


def draw_merge_proj(key, part):
    drawn = jnp.clip(jax.random.normal(jax.random.fold_in(key, 31), (MERGED, OUTW), jnp.float32), -6.0, 6.0)
    spread = 0.5
    column = jnp.clip(jax.random.normal(jax.random.fold_in(key, 32), (OUTW,), jnp.float32), -4.0, 4.0) * (spread / D)
    along = jnp.tile(direction(), 4)
    weight = drawn * MERGED ** (-0.5) + along[:, None] * column[None, :]
    return weight.astype(jnp.bfloat16)


def level_of(key, dims, pieces, low, top_value):
    level, own = 1.0, jax.random.fold_in(key, 6)
    for axis_at, blocks in pieces:
        draws = jnp.exp(jax.random.uniform(jax.random.fold_in(own, axis_at), (blocks,), jnp.float32, low / len(pieces), top_value / len(pieces)))
        level = level * jnp.repeat(draws, dims[axis_at] // blocks).reshape([-1 if axis == axis_at else 1 for axis in range(len(dims))])
    return level


def profile(count, total, most, skew):
    portions = [(1 << 20) // math.isqrt(standing ** skew) + 1 for standing in range(2, count + 1)]
    surplus, counts = total - most - (count - 1), [1] * (count - 1)
    while surplus > 0:
        free = [i for i in range(count - 1) if counts[i] < most]
        mass, budget = sum([portions[i] for i in free]), surplus
        for i in free:
            extra = min(most - counts[i], max(1, budget * portions[i] // mass), surplus)
            counts[i] = counts[i] + extra
            surplus = surplus - extra
    return np.array([most] + counts)


def ragged(own_key, number_of, total, limit, lean):
    if number_of == 2:
        one = jax.random.randint(own_key, (), max(1, total - limit), min(limit, total - 1) + 1)
        return jnp.stack([one, total - one])
    tallies = jnp.asarray(profile(number_of, total, limit, lean), jnp.int32)
    pairs = (number_of - 1) // 2
    source_of, sink = tallies[1:1 + 2 * pairs:2], tallies[2:2 + 2 * pairs:2]
    margin = jnp.minimum(source_of - 1, limit - sink)
    passed = jax.random.randint(jax.random.fold_in(own_key, 1), (pairs,), 0, 1 << 20) % (margin + 1)
    tallies = tallies.at[1:1 + 2 * pairs:2].set(source_of - passed).at[2:2 + 2 * pairs:2].set(sink + passed)
    return tallies[jax.random.permutation(jax.random.fold_in(own_key, 2), number_of)]


def deal_out(own_key, own, number, rows, number_of, top, reach, lean):
    order = jax.random.permutation(own_key, number_of)
    heavy_load, common = load_shares(number_of, rows * top, reach, lean, True), load_shares(number_of, rows * top, reach, lean, False)
    places = jnp.arange(number_of)

    def named(tallies, rotation):
        used = int((tallies > 0).sum())
        fixed = max(1, used // 4)
        passed = fixed + (places - fixed + rotation * (used - fixed)) % max(1, number_of - fixed)
        return jnp.zeros((number_of,), jnp.int32).at[order[jnp.where(places < fixed, places, passed)]].set(jnp.asarray(tallies, jnp.int32))

    tallies = jnp.where(number % 4 == 0, named(heavy_load, number // 4), named(common, number - number // 4 - 1))
    mixed = jax.random.permutation(jax.random.fold_in(own, 3), number_of)
    donor, taker = mixed[0:number_of // 2 * 2:2], mixed[1:number_of // 2 * 2:2]
    slack = jnp.minimum(tallies[donor] - 1, reach - tallies[taker]) // 2
    slack = jnp.where((donor == order[0]) | (taker == order[0]) | (tallies[taker] == 0), 0, jnp.maximum(slack, 0))
    passed = jax.random.randint(jax.random.fold_in(own, 4), (number_of // 2,), 0, 1 << 20) % (slack + 1)
    tallies = tallies.at[donor].add(-passed).at[taker].add(passed)
    members = jnp.searchsorted(jnp.cumsum(tallies), jnp.arange(rows * top), side="right").astype(jnp.int32)
    listing = members.reshape(top, rows).T
    listing = listing[jax.random.permutation(jax.random.fold_in(own, 1), rows)]
    rotation = jax.random.randint(jax.random.fold_in(own, 2), (rows, 1), 0, top)
    return jnp.take_along_axis(listing, (jnp.arange(top)[None, :] + rotation) % top, axis=1)


def load_shares(number_of, total, limit, slope, full):
    weights = [(1 << 20) // math.isqrt(rank ** slope) + 1 for rank in range(1, number_of + 1)]
    largest = limit if full else min(limit, max(-(-total // number_of), total * weights[0] // sum(weights)))
    least = 1 if total - largest >= number_of - 1 else 0
    counts, rest = [largest] + [least] * (number_of - 1), total - largest - least * (number_of - 1)
    while rest > 0:
        movable = [i for i in range(1, number_of) if counts[i] < largest] or [i for i in range(1, number_of) if counts[i] < limit]
        whole, budget = sum([weights[i] for i in movable]), rest
        for i in movable:
            more = min(limit - counts[i], max(1, budget * weights[i] // whole), rest)
            counts[i] = counts[i] + more
            rest = rest - more
    return np.array(counts)


def scatter_about(rng, extent, scale, reach, pieces=(), kind=jnp.bfloat16):
    result = jax.random.normal(rng, extent, jnp.float32) * scale
    if len(pieces) > 0:
        result = level_of(rng, extent, pieces, -0.22, 0.18) * result
    return jnp.clip(result, min=-reach, max=reach).astype(kind)


def setup_inputs(seed: int = 0, part: int = 0) -> dict:
    key_list = jax.random.split(jax.random.key(seed), 11)
    own_keys = jax.random.split(jax.random.fold_in(key_list[10], part), 11)
    queries = draw_queries(jax.random.fold_in(jax.random.fold_in(key_list[10], part), 71), part)
    keys = draw_keys(jax.random.fold_in(jax.random.fold_in(key_list[10], part), 71), part)
    values = scatter_about(own_keys[2], (TOKENS, D), 1.0, 6.0, ((0, 8),))
    residual_in = draw_residual_in(jax.random.fold_in(jax.random.fold_in(key_list[10], part), 71), part)
    out_proj = scatter_about(key_list[4], (D, D), D ** -0.5, 0.15625)
    ln_gain = jnp.clip(1.0 + 0.18 * jax.random.normal(key_list[5], (D,), jnp.float32), 0.1, 1.9)
    merge_proj = draw_merge_proj(jax.random.fold_in(key_list[10], 71), part)
    out_gain = jnp.clip(1.0 + 0.18 * jax.random.normal(key_list[7], (OUTW,), jnp.float32), 0.1, 1.9)
    image_rows = ragged(own_keys[8], NIMG, MROWS, REACH * MROW_DEV, 1).astype(jnp.int32)
    owners_keys = jax.random.split(jax.random.fold_in(own_keys[9], 1), MROWS // MROW_DEV)
    owners_turns = jax.random.permutation(jax.random.fold_in(own_keys[9], 3), MROWS // MROW_DEV)
    owners = jax.vmap(lambda own, number: deal_out(jax.random.fold_in(own_keys[9], 2), own, number, MROW_DEV, N_BLK, 1, CAP, 2))(owners_keys, owners_turns).reshape((MROWS, 1))
    return {"queries": queries, "keys": keys, "values": values, "residual_in": residual_in, "out_proj": out_proj, "ln_gain": ln_gain, "merge_proj": merge_proj, "out_gain": out_gain, "image_rows": image_rows, "owners": owners}


def image_of_rows(image_rows, count):
    ends = jnp.cumsum(image_rows)
    rows = jnp.arange(count, dtype=jnp.int32)
    return lax.optimization_barrier(jnp.sum((rows[:, None] >= ends[None, :]).astype(jnp.int32), axis=1)).astype(jnp.int32)

def reference(queries, keys, values, residual_in, out_proj, ln_gain, merge_proj, out_gain, image_rows, owners):
    row_image = image_of_rows(image_rows, MROWS)
    token_image = jnp.repeat(row_image, 4)
    scale = 1.0 / HDIM ** 0.5
    q_heads = queries.reshape(TOKENS, HEADS, HDIM).transpose(1, 0, 2)
    k_heads = keys.reshape(TOKENS, HEADS, HDIM).transpose(1, 0, 2)
    v_heads = values.reshape(TOKENS, HEADS, HDIM).transpose(1, 0, 2)
    same = token_image[:, None] == token_image[None, :]

    def one_head(parts):
        q_head, k_head, v_head = parts
        scores = jnp.dot(q_head, k_head.T, preferred_element_type=jnp.float32) * scale
        scores = jnp.where(same, scores, -jnp.inf)
        top = lax.optimization_barrier(jnp.max(scores, axis=1, keepdims=True))
        weights = jnp.exp(scores - top)
        total = lax.optimization_barrier(jnp.sum(weights, axis=1, keepdims=True))
        out = jnp.dot(weights.astype(jnp.bfloat16), v_head, preferred_element_type=jnp.float32) / total
        return out.astype(jnp.bfloat16)
    heads_out = lax.map(one_head, (q_heads, k_heads, v_heads))
    attended = heads_out.transpose(1, 0, 2).reshape(TOKENS, D)
    stream = residual_in.astype(jnp.float32) + jnp.dot(attended, out_proj, preferred_element_type=jnp.float32)
    mean = lax.optimization_barrier(jnp.mean(stream, axis=1, keepdims=True))
    centred = stream - mean
    var = lax.optimization_barrier(jnp.mean(centred * centred, axis=1, keepdims=True))
    normed = (centred * lax.rsqrt(var + 1e-06) * ln_gain[None, :]).astype(jnp.bfloat16)
    merged = normed.reshape(MROWS, MERGED)
    groups = merged.reshape(MROWS, N_BLK, FEAT_DEV).transpose(1, 0, 2)
    weight_groups = merge_proj.reshape(N_BLK, FEAT_DEV, OUTW)

    def add_group(carry, parts):
        feats, weight = parts
        partial_sum = jnp.dot(feats, weight, preferred_element_type=jnp.float32).astype(jnp.bfloat16)
        partial_sum = lax.optimization_barrier(partial_sum)
        return (carry + partial_sum.astype(jnp.float32), None)
    projected, unused = lax.scan(add_group, jnp.zeros((MROWS, OUTW), jnp.float32), (groups, weight_groups))
    row_squares = lax.optimization_barrier(jnp.sum(projected * projected, axis=1))
    member = (row_image[:, None] == jnp.arange(NIMG, dtype=jnp.int32)[None, :]).astype(jnp.float32)
    image_sums = lax.optimization_barrier(jnp.sum(member * row_squares[:, None], axis=0))
    image_mean = image_sums / (image_rows.astype(jnp.float32) * OUTW)
    row_scale = lax.rsqrt(image_mean + 1e-06)[row_image]
    scaled = (projected * row_scale[:, None] * out_gain[None, :]).astype(jnp.bfloat16)
    owner = owners[:, 0].astype(jnp.int32)
    source = (jnp.arange(MROWS, dtype=jnp.int32) // MROW_DEV).astype(jnp.int32)
    onehot = (owner[:, None] == jnp.arange(N_BLK, dtype=jnp.int32)[None, :]).astype(jnp.int32)
    running = jnp.cumsum(onehot.reshape(N_BLK, MROW_DEV, N_BLK), axis=1).reshape(MROWS, N_BLK)
    rank = lax.optimization_barrier(jnp.sum(running * onehot, axis=1)).astype(jnp.int32) - 1
    target = (owner * (N_BLK * CAP) + source * CAP + rank).astype(jnp.int32)
    delivered = jnp.zeros((N_BLK * N_BLK * CAP, OUTW), jnp.bfloat16).at[target].set(scaled)
    return delivered
```

```python
import jax
import jax.numpy as jnp
from jax import lax
from jax.experimental import pallas as pl
from jax.experimental.pallas import tpu as pltpu
from jax.sharding import PartitionSpec as P

MESH = pl.DeviceIdType.MESH
CHIPS = 4
PARTS = 2
LANES = 128

HEADS = 16


def passed_along(value, axis, steps):
    count = lax.axis_size(axis)
    first, last = (max(0, -steps), min(count, count - steps))
    return lax.ppermute(value, axis, [(source, source + steps) for source in range(first, last)])


def layer_norm(stream, gain):
    mean = jnp.mean(stream, axis=1, keepdims=True)
    centred = stream - mean
    var = jnp.mean(centred * centred, axis=1, keepdims=True)
    return centred * lax.rsqrt(var + 1e-06) * gain[None, :]


def tail_kernel(
    feats_in,
    weight_hbm,
    member_ref,
    slot_member,
    place_ref,
    gain_ref,
    count_ref,
    out_ref,
    weight,
    feats,
    keep,
    give,
    taken,
    moving,
    from_left,
    from_right,
    packed,
    landed,
    slot_images,
    sums,
    weight_sem,
    feat_sems,
    slot_sems,
    pair_sems,
    line_sems,
    deliver_sems,
    sum_sems,
):
    blocks, rows, depth = feats_in.shape
    parts, width = keep.shape[0], keep.shape[3]
    cap = slot_member.shape[1]
    me = lax.axis_index("blk")
    chip, core = me // 2, lax.rem(me, 2)
    sibling = me + 1 - 2 * core

    def send(src, dst, sems, index, landing, target):
        return pltpu.make_async_remote_copy(
            src_ref=src,
            dst_ref=dst,
            send_sem=sems.at[(0,) + index],
            recv_sem=sems.at[(1,) + landing],
            device_id={"blk": target},
            device_id_type=MESH,
        )

    weight_copy = pltpu.make_async_copy(weight_hbm, weight, weight_sem)
    weight_copy.start()

    barrier = pltpu.get_barrier_semaphore()
    others = [lax.rem(me + step, blocks) for step in (4, 5, 3, 6, 2, 7, 1)]
    for other in others:
        pl.semaphore_signal(barrier, inc=1, device_id={"blk": other}, device_id_type=MESH)
    pl.semaphore_wait(barrier, blocks - 1)

    for other in others:
        send(feats_in.at[other], feats.at[me], feat_sems, (other,), (me,), other).start()
    feats[me] = feats_in[me]
    for other in others:
        send(slot_member.at[other], slot_images.at[me], slot_sems, (other,), (me,), other).start()
    slot_images[me] = slot_member[me]
    weight_copy.wait()

    def place_in_order(step):
        far = jnp.maximum(chip, CHIPS - 1 - chip)
        swapped = jnp.where(far == CHIPS - 1, step, 2 * CHIPS - 3 - step)
        low = jnp.where(step < 2, step, swapped)
        return jnp.where(chip >= 2, low, CHIPS - 1 - low)

    def wait_feats(source):
        @pl.when(source != me)
        def _():
            send(feats_in.at[source], feats.at[source], feat_sems, (source,), (source,), source).wait_recv()

    tile = 1024

    def multiply(part, first):
        def one(step, unused):
            to = place_in_order(step)
            if first:
                wait_feats(2 * to)
                wait_feats(2 * to + 1)
            lhs = jnp.concatenate([feats[2 * to + 1 - core], feats[2 * to + core]], axis=0)
            for at in range(0, width, tile):
                product = jnp.dot(
                    lhs,
                    weight[:, pl.ds(part * width + at, tile)],
                    preferred_element_type=jnp.float32,
                ).astype(jnp.bfloat16)
                give[part, to, :, pl.ds(at, tile)] = product[:rows]
                keep[part, to, :, pl.ds(at, tile)] = product[rows:]
            send(give.at[part, to], taken.at[part, to], pair_sems, (part, to), (part, to), sibling).start()
            return unused

        lax.fori_loop(0, CHIPS, one, 0)

    def pair_sum(part, to):
        send(give.at[part, to], taken.at[part, to], pair_sems, (part, to), (part, to), sibling).wait_recv()

    def pass_on(part, to, arrivals, direction, edge, way):
        pair_sum(part, to)

        @pl.when(edge)
        def _():
            moving[part, to] = (
                keep[part, to].astype(jnp.float32) + taken[part, to].astype(jnp.float32)
            ).astype(jnp.bfloat16)

        @pl.when(jnp.logical_not(edge))
        def _():
            line_copy(part, to, arrivals, way, direction).wait_recv()
            moving[part, to] = (
                keep[part, to].astype(jnp.float32)
                + taken[part, to].astype(jnp.float32)
                + arrivals[part, to].astype(jnp.float32)
            ).astype(jnp.bfloat16)

        line_copy(part, to, arrivals, way, direction).start()

    def line_copy(part, to, arrivals, way, direction):
        target = jnp.clip(me + direction, 0, blocks - 1)
        return pltpu.make_async_remote_copy(
            src_ref=moving.at[part, to],
            dst_ref=arrivals.at[part, to],
            send_sem=line_sems.at[0, part, to],
            recv_sem=line_sems.at[way, part, to],
            device_id={"blk": target},
            device_id_type=MESH,
        )

    def line_step(part, distance):
        @pl.when(chip + distance < CHIPS)
        def _():
            pass_on(part, chip + distance, from_left, 2, chip == 0, 1)

        @pl.when(chip - distance >= 0)
        def _():
            pass_on(part, chip - distance, from_right, -2, chip == CHIPS - 1, 2)

    def finish(part, squares):
        pair_sum(part, chip)

        @pl.when(chip > 0)
        def _():
            line_copy(part, chip, from_left, 1, 2).wait_recv()

        @pl.when(chip == 0)
        def _():
            from_left[part, chip] = jnp.zeros((rows, width), jnp.bfloat16)

        @pl.when(chip < CHIPS - 1)
        def _():
            line_copy(part, chip, from_right, 2, -2).wait_recv()

        @pl.when(chip == CHIPS - 1)
        def _():
            from_right[part, chip] = jnp.zeros((rows, width), jnp.bfloat16)

        step = 512
        for at in range(0, width, step):
            cols = pl.ds(at, step)
            total = (
                keep[part, chip, :, cols].astype(jnp.float32)
                + taken[part, chip, :, cols].astype(jnp.float32)
                + from_left[part, chip, :, cols].astype(jnp.float32)
                + from_right[part, chip, :, cols].astype(jnp.float32)
            )
            squares = squares + jnp.sum(total * total, axis=1, keepdims=True)
            slots = jnp.dot(
                place_ref[...], total.astype(jnp.bfloat16), preferred_element_type=jnp.float32
            ).astype(jnp.bfloat16)
            for owner in range(blocks):
                packed[part, owner, :, cols] = slots[owner * cap : (owner + 1) * cap]
        for other in others:
            send(packed.at[part, other], landed.at[part, me], deliver_sems, (part, other), (part, me), other).start()
        landed[part, me] = packed[part, me]
        return squares

    multiply(0, True)
    line_step(0, CHIPS - 1)
    for part in range(1, parts):
        multiply(part, False)
    for distance in range(CHIPS - 2, 0, -1):
        line_step(0, distance)
    squares = jnp.zeros((rows, 1), jnp.float32)
    for part in range(parts):
        if part + 1 < parts:
            for distance in range(CHIPS - 1, 0, -1):
                line_step(part + 1, distance)
        squares = finish(part, squares)

    mine = jnp.sum(member_ref[...] * squares, axis=0, keepdims=True)
    sums[me] = jnp.broadcast_to(mine, (8, LANES))
    for other in others:
        send(sums.at[me], sums.at[me], sum_sems, (other,), (me,), other).start()
    for other in others:
        send(sums.at[me], sums.at[other], sum_sems, (other,), (other,), other).wait_recv()
    total = sums[0]
    for source in range(1, blocks):
        total = total + sums[source]
    inverse = lax.rsqrt(total / count_ref[...] + 1e-06)[0:1]

    for step in range(blocks):
        source = me if step == 0 else others[blocks - 1 - step]
        if step:
            send(slot_member.at[source], slot_images.at[source], slot_sems, (source,), (source,), source).wait_recv()
        row_scale = jnp.sum(slot_images[source] * inverse, axis=1, keepdims=True)
        lines = pl.ds(pl.multiple_of(source * cap, cap), cap)
        for part in range(parts):
            if step:
                send(
                    packed.at[part, source], landed.at[part, source], deliver_sems, (part, source), (part, source), source
                ).wait_recv()
            out_ref[lines, pl.ds(part * width, width)] = (
                landed[part, source].astype(jnp.float32)
                * row_scale
                * gain_ref[:, pl.ds(part * width, width)]
            ).astype(jnp.bfloat16)

    for other in others:
        send(feats_in.at[other], feats.at[me], feat_sems, (other,), (me,), other).wait_send()
        send(slot_member.at[other], slot_images.at[me], slot_sems, (other,), (me,), other).wait_send()
        send(sums.at[me], sums.at[me], sum_sems, (other,), (me,), other).wait_send()
        for part in range(parts):
            send(packed.at[part, other], landed.at[part, me], deliver_sems, (part, other), (part, me), other).wait_send()
    for part in range(parts):
        for to in range(CHIPS):
            send(give.at[part, to], taken.at[part, to], pair_sems, (part, to), (part, to), sibling).wait_send()

            @pl.when(chip < to)
            def _():
                line_copy(part, to, from_left, 1, 2).wait_send()

            @pl.when(chip > to)
            def _():
                line_copy(part, to, from_right, 2, -2).wait_send()


def merged_tail(merged, merge_proj, out_gain, image_rows, owner, my_rows_img, blocks):
    rows = merged.shape[0]
    depth, out_width = merge_proj.shape
    nimg = image_rows.shape[0]
    cap = max(2, 2 * rows // blocks)
    width = out_width // PARTS
    feats_in = merged.reshape(rows, blocks, depth).transpose(1, 0, 2)
    lanes = jnp.arange(LANES, dtype=jnp.int32)
    member = (my_rows_img[:, None] == lanes[None, :]).astype(jnp.float32)
    onehot = (owner[:, None] == jnp.arange(blocks, dtype=jnp.int32)[None, :]).astype(jnp.int32)
    rank = jnp.sum(jnp.cumsum(onehot, axis=0) * onehot, axis=1) - 1
    slot = owner * cap + rank
    filled = jnp.arange(blocks * cap, dtype=jnp.int32)[:, None] == slot[None, :]
    place = filled.astype(jnp.bfloat16)
    slot_img = jnp.sum(jnp.where(filled, my_rows_img[None, :] + 1, 0), axis=1) - 1
    slot_member = (slot_img[:, None] == lanes[None, :]).astype(jnp.float32)
    slot_member = slot_member.reshape(blocks, cap, LANES)
    counts = jnp.ones((LANES,), jnp.float32).at[:nimg].set(
        image_rows.astype(jnp.float32) * out_width
    )
    counts = jnp.broadcast_to(counts[None, :], (8, LANES))
    vmem = pl.BlockSpec(memory_space=pltpu.VMEM)
    tiles = (PARTS, CHIPS, rows, width)
    half = jnp.bfloat16
    return pl.pallas_call(
        tail_kernel,
        out_shape=jax.ShapeDtypeStruct((blocks * cap, out_width), half),
        in_specs=[vmem, pl.BlockSpec(memory_space=pl.ANY)] + [vmem] * 5,
        out_specs=vmem,
        scratch_shapes=[
            pltpu.VMEM((depth, out_width), half),
            pltpu.VMEM((blocks, rows, depth), half),
            pltpu.VMEM(tiles, half),
            pltpu.VMEM(tiles, half),
            pltpu.VMEM(tiles, half),
            pltpu.VMEM(tiles, half),
            pltpu.VMEM(tiles, half),
            pltpu.VMEM(tiles, half),
            pltpu.VMEM((PARTS, blocks, cap, width), half),
            pltpu.VMEM((PARTS, blocks, cap, width), half),
            pltpu.VMEM((blocks, cap, LANES), jnp.float32),
            pltpu.VMEM((blocks, 8, LANES), jnp.float32),
            pltpu.SemaphoreType.DMA,
            pltpu.SemaphoreType.DMA((2, blocks)),
            pltpu.SemaphoreType.DMA((2, blocks)),
            pltpu.SemaphoreType.DMA((2, PARTS, CHIPS)),
            pltpu.SemaphoreType.DMA((3, PARTS, CHIPS)),
            pltpu.SemaphoreType.DMA((2, PARTS, blocks)),
            pltpu.SemaphoreType.DMA((2, blocks)),
        ],
        compiler_params=pltpu.CompilerParams(
            collective_id=0, has_side_effects=True, vmem_limit_bytes=44 * 1024 * 1024
        ),
        cost_estimate=pl.CostEstimate(
            flops=2 * rows * blocks * depth * out_width,
            bytes_accessed=2 * depth * out_width,
            transcendentals=0,
        ),
    )(feats_in, merge_proj, member, slot_member, place, out_gain[None, :], counts)


def on_device(
    queries, keys, values, residual_in, out_proj, ln_gain, merge_proj, out_gain, image_rows, owners
):
    blocks = lax.axis_size("blk")
    me_index = lax.axis_index("blk")
    tok, width = queries.shape
    row_count = tok // 4
    heads = HEADS
    hdim = width // heads
    reach = min(6, (blocks - 1) // 2)
    scale = 1.0 / hdim**0.5
    ends = jnp.cumsum(image_rows)

    def images_of(source, rows):
        found = jnp.sum((rows[:, None] >= ends[None, :]).astype(jnp.int32), axis=1)
        inside = jnp.logical_and(source >= 0, source < blocks)
        return jnp.where(inside, found, -1)

    def row_images(source):
        return images_of(source, source * row_count + jnp.arange(row_count, dtype=jnp.int32))

    def token_images(source):
        return images_of(source, source * row_count + jnp.arange(tok, dtype=jnp.int32) // 4)

    query_img = token_images(me_index)
    q_heads = queries.reshape(tok, heads, hdim)
    own_pair = jnp.stack([keys, values])

    def masked_scores(pair, key_img):
        k_heads = pair[0].reshape(-1, heads, hdim)
        scores = (
            jnp.einsum("qhd,khd->hqk", q_heads, k_heads, preferred_element_type=jnp.float32) * scale
        )
        return jnp.where(query_img[None, :, None] == key_img[None, None, :], scores, -jnp.inf)

    def weigh_values(weights, pair):
        v_heads = pair[1].reshape(-1, heads, hdim)
        return jnp.einsum(
            "hqk,khd->hqd",
            weights.astype(jnp.bfloat16),
            v_heads,
            preferred_element_type=jnp.float32,
        )

    def absorb(state, pair, key_img):

        def update(carry):
            running_max, running_sum, accum = carry
            scores = masked_scores(pair, key_img)
            new_max = jnp.maximum(running_max, jnp.max(scores, axis=2, keepdims=True))
            factor = jnp.exp(running_max - new_max)
            weights = jnp.exp(scores - new_max)
            new_sum = running_sum * factor + jnp.sum(weights, axis=2, keepdims=True)
            new_accum = accum * factor + weigh_values(weights, pair)
            return (new_max, new_sum, new_accum)

        live = jnp.logical_and(
            jnp.max(key_img) >= jnp.maximum(jnp.min(query_img), 0),
            jnp.min(jnp.where(key_img >= 0, key_img, 1 << 30)) <= jnp.max(query_img),
        )
        return lax.cond(live, update, lambda carry: carry, state)

    first_scores = masked_scores(own_pair, query_img)
    first_max = jnp.max(first_scores, axis=2, keepdims=True)
    first_weights = jnp.exp(first_scores - first_max)
    state = (
        first_max,
        jnp.sum(first_weights, axis=2, keepdims=True),
        weigh_values(first_weights, own_pair),
    )
    from_left = own_pair
    from_right = own_pair
    for step in range(1, reach + 1):
        from_left = passed_along(from_left, "blk", 1)
        state = absorb(state, from_left, token_images(me_index - step))
        from_right = passed_along(from_right, "blk", -1)
        state = absorb(state, from_right, token_images(me_index + step))
    heads_out = state[2] / state[1]
    attended = heads_out.transpose(1, 0, 2).reshape(tok, width).astype(jnp.bfloat16)
    stream = residual_in.astype(jnp.float32) + jnp.dot(
        attended, out_proj, preferred_element_type=jnp.float32
    )
    normed = layer_norm(stream, ln_gain).astype(jnp.bfloat16)
    merged = normed.reshape(row_count, 4 * width)
    if blocks == 2 * CHIPS:
        return merged_tail(
            merged, merge_proj, out_gain, image_rows, owners[:, 0], row_images(me_index), blocks
        )
    feature_rows = lax.all_to_all(merged, "blk", split_axis=1, concat_axis=0, tiled=True)
    projected = lax.psum_scatter(
        jnp.dot(feature_rows, merge_proj, preferred_element_type=jnp.float32).astype(jnp.bfloat16),
        "blk",
        scatter_dimension=0,
        tiled=True,
    ).astype(jnp.float32)
    my_rows_img = row_images(me_index)
    nimg = image_rows.shape[0]
    member = (my_rows_img[:, None] == jnp.arange(nimg, dtype=jnp.int32)[None, :]).astype(
        jnp.float32
    )
    row_squares = jnp.sum(projected * projected, axis=1)
    image_sums = lax.psum(jnp.sum(member * row_squares[:, None], axis=0), "blk")
    out_width = projected.shape[1]
    image_mean = image_sums / (image_rows.astype(jnp.float32) * out_width)
    row_scale = jnp.sum(member * lax.rsqrt(image_mean + 1e-06)[None, :], axis=1)
    scaled = (projected * row_scale[:, None] * out_gain[None, :]).astype(jnp.bfloat16)
    capacity = max(2, 2 * row_count // blocks)
    owner = owners[:, 0]
    onehot = (owner[:, None] == jnp.arange(blocks, dtype=jnp.int32)[None, :]).astype(jnp.int32)
    rank = jnp.sum(jnp.cumsum(onehot, axis=0) * onehot, axis=1) - 1
    slot = owner * capacity + rank
    placement = (jnp.arange(blocks * capacity, dtype=jnp.int32)[:, None] == slot[None, :]).astype(
        jnp.bfloat16
    )
    outgoing = jnp.dot(placement, scaled, preferred_element_type=jnp.float32).astype(jnp.bfloat16)
    return lax.all_to_all(outgoing, "blk", split_axis=0, concat_axis=0, tiled=True)


def solution(mesh):
    in_specs = (
        P(("dp", "blk"), None),
        P(("dp", "blk"), None),
        P(("dp", "blk"), None),
        P(("dp", "blk"), None),
        P(),
        P(),
        P("blk", None),
        P(),
        P("dp"),
        P(("dp", "blk"), None),
    )
    out_specs = P(("dp", "blk"), None)
    return jax.shard_map(
        on_device, mesh=mesh, in_specs=in_specs, out_specs=out_specs, check_vma=False
    )
```

```python
import functools

import jax
import jax.numpy as jnp
from jax import lax
from jax.experimental import pallas as pl
from jax.experimental.pallas import tpu as pltpu
from jax.sharding import PartitionSpec as P

MESH = pl.DeviceIdType.MESH
CHIPS = 4
PARTS = 2
LANES = 128

HEADS = 16


def passed_along(value, axis, steps):
    count = lax.axis_size(axis)
    first, last = (max(0, -steps), min(count, count - steps))
    return lax.ppermute(value, axis, [(source, source + steps) for source in range(first, last)])


def layer_norm(stream, gain):
    mean = jnp.mean(stream, axis=1, keepdims=True)
    centred = stream - mean
    var = jnp.mean(centred * centred, axis=1, keepdims=True)
    return centred * lax.rsqrt(var + 1e-06) * gain[None, :]


def tail_kernel(
    feats_in,
    weight_hbm,
    member_ref,
    slot_member,
    place_ref,
    gain_ref,
    count_ref,
    out_ref,
    weight,
    feats,
    keep,
    give,
    taken,
    moving,
    from_left,
    from_right,
    packed,
    landed,
    slot_images,
    sums,
    weight_sem,
    feat_sems,
    slot_sems,
    pair_sems,
    line_sems,
    deliver_sems,
    sum_sems,
):
    blocks, rows, depth = feats_in.shape
    parts, width = keep.shape[0], keep.shape[3]
    cap = slot_member.shape[1]
    me = lax.axis_index("blk")
    chip, core = me // 2, lax.rem(me, 2)
    sibling = me + 1 - 2 * core

    def send(src, dst, sems, index, landing, target):
        return pltpu.make_async_remote_copy(
            src_ref=src,
            dst_ref=dst,
            send_sem=sems.at[(0,) + index],
            recv_sem=sems.at[(1,) + landing],
            device_id={"blk": target},
            device_id_type=MESH,
        )

    weight_copy = pltpu.make_async_copy(weight_hbm, weight, weight_sem)
    weight_copy.start()

    barrier = pltpu.get_barrier_semaphore()
    others = [lax.rem(me + step, blocks) for step in (4, 5, 3, 6, 2, 7, 1)]
    for other in others:
        pl.semaphore_signal(barrier, inc=1, device_id={"blk": other}, device_id_type=MESH)
    pl.semaphore_wait(barrier, blocks - 1)

    for other in others:
        send(feats_in.at[other], feats.at[me], feat_sems, (other,), (me,), other).start()
    feats[me] = feats_in[me]
    for other in others:
        send(slot_member.at[other], slot_images.at[me], slot_sems, (other,), (me,), other).start()
    slot_images[me] = slot_member[me]
    weight_copy.wait()

    def place_in_order(step):
        far = jnp.maximum(chip, CHIPS - 1 - chip)
        swapped = jnp.where(far == CHIPS - 1, step, 2 * CHIPS - 3 - step)
        low = jnp.where(step < 2, step, swapped)
        return jnp.where(chip >= 2, low, CHIPS - 1 - low)

    def wait_feats(source):
        @pl.when(source != me)
        def _():
            send(feats_in.at[source], feats.at[source], feat_sems, (source,), (source,), source).wait_recv()

    tile = 1024

    def multiply(part, first):
        def one(step, unused):
            to = place_in_order(step)
            if first:
                wait_feats(2 * to)
                wait_feats(2 * to + 1)
            lhs = jnp.concatenate([feats[2 * to + 1 - core], feats[2 * to + core]], axis=0)
            for at in range(0, width, tile):
                product = jnp.dot(
                    lhs,
                    weight[:, pl.ds(part * width + at, tile)],
                    preferred_element_type=jnp.float32,
                ).astype(jnp.bfloat16)
                give[part, to, :, pl.ds(at, tile)] = product[:rows]
                keep[part, to, :, pl.ds(at, tile)] = product[rows:]
            send(give.at[part, to], taken.at[part, to], pair_sems, (part, to), (part, to), sibling).start()
            return unused

        lax.fori_loop(0, CHIPS, one, 0)

    def pair_sum(part, to):
        send(give.at[part, to], taken.at[part, to], pair_sems, (part, to), (part, to), sibling).wait_recv()

    def pass_on(part, to, arrivals, direction, edge, way):
        pair_sum(part, to)

        @pl.when(edge)
        def _():
            moving[part, to] = (
                keep[part, to].astype(jnp.float32) + taken[part, to].astype(jnp.float32)
            ).astype(jnp.bfloat16)

        @pl.when(jnp.logical_not(edge))
        def _():
            line_copy(part, to, arrivals, way, direction).wait_recv()
            moving[part, to] = (
                keep[part, to].astype(jnp.float32)
                + taken[part, to].astype(jnp.float32)
                + arrivals[part, to].astype(jnp.float32)
            ).astype(jnp.bfloat16)

        line_copy(part, to, arrivals, way, direction).start()

    def line_copy(part, to, arrivals, way, direction):
        target = jnp.clip(me + direction, 0, blocks - 1)
        return pltpu.make_async_remote_copy(
            src_ref=moving.at[part, to],
            dst_ref=arrivals.at[part, to],
            send_sem=line_sems.at[0, part, to],
            recv_sem=line_sems.at[way, part, to],
            device_id={"blk": target},
            device_id_type=MESH,
        )

    def line_step(part, distance):
        @pl.when(chip + distance < CHIPS)
        def _():
            pass_on(part, chip + distance, from_left, 2, chip == 0, 1)

        @pl.when(chip - distance >= 0)
        def _():
            pass_on(part, chip - distance, from_right, -2, chip == CHIPS - 1, 2)

    def finish(part, squares):
        pair_sum(part, chip)

        @pl.when(chip > 0)
        def _():
            line_copy(part, chip, from_left, 1, 2).wait_recv()

        @pl.when(chip == 0)
        def _():
            from_left[part, chip] = jnp.zeros((rows, width), jnp.bfloat16)

        @pl.when(chip < CHIPS - 1)
        def _():
            line_copy(part, chip, from_right, 2, -2).wait_recv()

        @pl.when(chip == CHIPS - 1)
        def _():
            from_right[part, chip] = jnp.zeros((rows, width), jnp.bfloat16)

        step = 512
        for at in range(0, width, step):
            cols = pl.ds(at, step)
            total = (
                keep[part, chip, :, cols].astype(jnp.float32)
                + taken[part, chip, :, cols].astype(jnp.float32)
                + from_left[part, chip, :, cols].astype(jnp.float32)
                + from_right[part, chip, :, cols].astype(jnp.float32)
            )
            squares = squares + jnp.sum(total * total, axis=1, keepdims=True)
            slots = jnp.dot(
                place_ref[...], total.astype(jnp.bfloat16), preferred_element_type=jnp.float32
            ).astype(jnp.bfloat16)
            for owner in range(blocks):
                packed[part, owner, :, cols] = slots[owner * cap : (owner + 1) * cap]
        for other in others:
            send(packed.at[part, other], landed.at[part, me], deliver_sems, (part, other), (part, me), other).start()
        landed[part, me] = packed[part, me]
        return squares

    multiply(0, True)
    line_step(0, CHIPS - 1)
    for part in range(1, parts):
        multiply(part, False)
    for distance in range(CHIPS - 2, 0, -1):
        line_step(0, distance)
    squares = jnp.zeros((rows, 1), jnp.float32)
    for part in range(parts):
        if part + 1 < parts:
            for distance in range(CHIPS - 1, 0, -1):
                line_step(part + 1, distance)
        squares = finish(part, squares)

    mine = jnp.sum(member_ref[...] * squares, axis=0, keepdims=True)
    sums[me] = jnp.broadcast_to(mine, (8, LANES))
    for other in others:
        send(sums.at[me], sums.at[me], sum_sems, (other,), (me,), other).start()
    for other in others:
        send(sums.at[me], sums.at[other], sum_sems, (other,), (other,), other).wait_recv()
    total = sums[0]
    for source in range(1, blocks):
        total = total + sums[source]
    inverse = lax.rsqrt(total / count_ref[...] + 1e-06)[0:1]

    for step in range(blocks):
        source = me if step == 0 else others[blocks - 1 - step]
        if step:
            send(slot_member.at[source], slot_images.at[source], slot_sems, (source,), (source,), source).wait_recv()
        row_scale = jnp.sum(slot_images[source] * inverse, axis=1, keepdims=True)
        lines = pl.ds(pl.multiple_of(source * cap, cap), cap)
        for part in range(parts):
            if step:
                send(
                    packed.at[part, source], landed.at[part, source], deliver_sems, (part, source), (part, source), source
                ).wait_recv()
            out_ref[lines, pl.ds(part * width, width)] = (
                landed[part, source].astype(jnp.float32)
                * row_scale
                * gain_ref[:, pl.ds(part * width, width)]
            ).astype(jnp.bfloat16)

    for other in others:
        send(feats_in.at[other], feats.at[me], feat_sems, (other,), (me,), other).wait_send()
        send(slot_member.at[other], slot_images.at[me], slot_sems, (other,), (me,), other).wait_send()
        send(sums.at[me], sums.at[me], sum_sems, (other,), (me,), other).wait_send()
        for part in range(parts):
            send(packed.at[part, other], landed.at[part, me], deliver_sems, (part, other), (part, me), other).wait_send()
    for part in range(parts):
        for to in range(CHIPS):
            send(give.at[part, to], taken.at[part, to], pair_sems, (part, to), (part, to), sibling).wait_send()

            @pl.when(chip < to)
            def _():
                line_copy(part, to, from_left, 1, 2).wait_send()

            @pl.when(chip > to)
            def _():
                line_copy(part, to, from_right, 2, -2).wait_send()


def merged_tail(feats_in, merge_proj, out_gain, image_rows, owner, my_rows_img, blocks):
    rows = feats_in.shape[1]
    depth, out_width = merge_proj.shape
    nimg = image_rows.shape[0]
    cap = max(2, 2 * rows // blocks)
    width = out_width // PARTS
    lanes = jnp.arange(LANES, dtype=jnp.int32)
    member = (my_rows_img[:, None] == lanes[None, :]).astype(jnp.float32)
    onehot = (owner[:, None] == jnp.arange(blocks, dtype=jnp.int32)[None, :]).astype(jnp.int32)
    rank = jnp.sum(jnp.cumsum(onehot, axis=0) * onehot, axis=1) - 1
    slot = owner * cap + rank
    filled = jnp.arange(blocks * cap, dtype=jnp.int32)[:, None] == slot[None, :]
    place = filled.astype(jnp.bfloat16)
    slot_img = jnp.sum(jnp.where(filled, my_rows_img[None, :] + 1, 0), axis=1) - 1
    slot_member = (slot_img[:, None] == lanes[None, :]).astype(jnp.float32)
    slot_member = slot_member.reshape(blocks, cap, LANES)
    counts = jnp.ones((LANES,), jnp.float32).at[:nimg].set(
        image_rows.astype(jnp.float32) * out_width
    )
    counts = jnp.broadcast_to(counts[None, :], (8, LANES))
    vmem = pl.BlockSpec(memory_space=pltpu.VMEM)
    tiles = (PARTS, CHIPS, rows, width)
    half = jnp.bfloat16
    return pl.pallas_call(
        tail_kernel,
        out_shape=jax.ShapeDtypeStruct((blocks * cap, out_width), half),
        in_specs=[vmem, pl.BlockSpec(memory_space=pl.ANY)] + [vmem] * 5,
        out_specs=vmem,
        scratch_shapes=[
            pltpu.VMEM((depth, out_width), half),
            pltpu.VMEM((blocks, rows, depth), half),
            pltpu.VMEM(tiles, half),
            pltpu.VMEM(tiles, half),
            pltpu.VMEM(tiles, half),
            pltpu.VMEM(tiles, half),
            pltpu.VMEM(tiles, half),
            pltpu.VMEM(tiles, half),
            pltpu.VMEM((PARTS, blocks, cap, width), half),
            pltpu.VMEM((PARTS, blocks, cap, width), half),
            pltpu.VMEM((blocks, cap, LANES), jnp.float32),
            pltpu.VMEM((blocks, 8, LANES), jnp.float32),
            pltpu.SemaphoreType.DMA,
            pltpu.SemaphoreType.DMA((2, blocks)),
            pltpu.SemaphoreType.DMA((2, blocks)),
            pltpu.SemaphoreType.DMA((2, PARTS, CHIPS)),
            pltpu.SemaphoreType.DMA((3, PARTS, CHIPS)),
            pltpu.SemaphoreType.DMA((2, PARTS, blocks)),
            pltpu.SemaphoreType.DMA((2, blocks)),
        ],
        compiler_params=pltpu.CompilerParams(
            collective_id=0, has_side_effects=True, vmem_limit_bytes=44 * 1024 * 1024
        ),
        cost_estimate=pl.CostEstimate(
            flops=2 * rows * blocks * depth * out_width,
            bytes_accessed=2 * depth * out_width,
            transcendentals=0,
        ),
    )(feats_in, merge_proj, member, slot_member, place, out_gain[None, :], counts)


def attend_kernel(
    reach,
    q_ref,
    k_ref,
    v_ref,
    res_ref,
    proj_hbm,
    gain_ref,
    query_img,
    key_img,
    out_ref,
    proj,
    from_left,
    from_right,
    q_heads,
    tops,
    totals,
    accum,
    bias,
    attended,
    stream,
    tiles,
    proj_sem,
    right_sems,
    left_sems,
):
    tok, width = q_ref.shape
    hdim = width // HEADS
    blocks = lax.axis_size("blk")
    me = lax.axis_index("blk")
    scale = 1.4426950408889634 / hdim**0.5

    proj_copy = pltpu.make_async_copy(proj_hbm, proj, proj_sem)
    proj_copy.start()

    barrier = pltpu.get_barrier_semaphore()

    @pl.when(me > 0)
    def _():
        pl.semaphore_signal(barrier, inc=1, device_id={"blk": me - 1}, device_id_type=MESH)

    @pl.when(me < blocks - 1)
    def _():
        pl.semaphore_signal(barrier, inc=1, device_id={"blk": me + 1}, device_id_type=MESH)

    at_end = jnp.logical_or(me == 0, me == blocks - 1)

    @pl.when(at_end)
    def _():
        pl.semaphore_wait(barrier, 1)

    @pl.when(jnp.logical_not(at_end))
    def _():
        pl.semaphore_wait(barrier, 2)

    def pair_copies(step, buffers, sems, direction):
        target = jnp.clip(me + direction, 0, blocks - 1)
        found = []
        for which, own in ((0, k_ref), (1, v_ref)):
            found.append(
                pltpu.make_async_remote_copy(
                    src_ref=own if step == 1 else buffers.at[step - 2, which],
                    dst_ref=buffers.at[step - 1, which],
                    send_sem=sems.at[0, step - 1, which],
                    recv_sem=sems.at[1, step - 1, which],
                    device_id={"blk": target},
                    device_id_type=MESH,
                )
            )
        return found

    ways = ((from_left, right_sems, 1), (from_right, left_sems, -1))

    def sends(step, direction):
        if direction > 0:
            return jnp.logical_and(me + 1 < blocks, me - step + 1 >= 0)
        return jnp.logical_and(me >= 1, me + step - 1 < blocks)

    def comes(step, direction):
        return me - step >= 0 if direction > 0 else me + step < blocks

    def start(step, way):
        @pl.when(sends(step, way[2]))
        def _():
            for copy in pair_copies(step, *way):
                copy.start()

    def wait_send(step, way):
        @pl.when(sends(step, way[2]))
        def _():
            for copy in pair_copies(step, *way):
                copy.wait_send()

    def wait_recv(step, way):
        @pl.when(comes(step, way[2]))
        def _():
            for copy in pair_copies(step, *way):
                copy.wait_recv()

    def window(head):
        return min(head * hdim // LANES, width // LANES - 2) * LANES

    def of_head(head):
        column = window(head) + lax.broadcasted_iota(jnp.int32, (tok, 2 * LANES), 1)
        return jnp.logical_and(column >= head * hdim, column < (head + 1) * hdim)

    def attend(k_at, v_at, images, first):
        bias[...] = jnp.where(query_img[...] == images, 0.0, -jnp.inf)
        for head in range(HEADS):
            cols = pl.ds(window(head), 2 * LANES)
            scores = (
                lax.dot_general(
                    q_heads[head],
                    k_at[:, cols],
                    (((1,), (1,)), ((), ())),
                    preferred_element_type=jnp.float32,
                )
                * scale
                + bias[...]
            )
            top = jnp.max(scores, axis=1, keepdims=True)
            if not first:
                before = tops[head]
                top = jnp.maximum(before, top)
                factor = jnp.exp2(before - top)
            weights = jnp.exp2(scores - top)
            total = jnp.sum(weights, axis=1, keepdims=True)
            found = jnp.dot(
                weights.astype(jnp.bfloat16), v_at[:, cols], preferred_element_type=jnp.float32
            )
            if not first:
                total = totals[head] * factor + total
                found = accum[head] * factor + found
            tops[head] = top
            totals[head] = total
            accum[head] = found

    for way in ways:
        start(1, way)
    for head in range(HEADS):
        cols = pl.ds(window(head), 2 * LANES)
        q_heads[head] = jnp.where(of_head(head), q_ref[:, cols], jnp.zeros((), jnp.bfloat16))
    attend(k_ref, v_ref, key_img[reach], True)
    for step in range(1, reach + 1):
        for way in ways:
            wait_recv(step, way)
            wait_send(step, way)
            if step < reach:
                start(step + 1, way)
        for buffers, _, direction in ways:

            @pl.when(comes(step, direction))
            def _():
                attend(
                    buffers.at[step - 1, 0],
                    buffers.at[step - 1, 1],
                    key_img[reach - direction * step],
                    False,
                )

    attended[...] = jnp.zeros((tok, width), jnp.bfloat16)
    for head in range(HEADS):
        cols = pl.ds(window(head), 2 * LANES)
        found = (accum[head] / totals[head]).astype(jnp.bfloat16)
        attended[:, cols] = jnp.where(of_head(head), found, attended[:, cols])

    proj_copy.wait()
    tile = 512
    for at in range(0, width, tile):
        cols = pl.ds(at, min(tile, width - at))
        stream[:, cols] = res_ref[:, cols].astype(jnp.float32) + jnp.dot(
            attended[...], proj[:, cols], preferred_element_type=jnp.float32
        )
    rows = tok // 4
    for at in range(0, tok, rows):
        lines = pl.ds(at, rows)
        normed = layer_norm(stream[lines, :], gain_ref[0])
        for tile in range(width // LANES):
            tiles[tile, lines, :] = normed[:, tile * LANES : (tile + 1) * LANES]
    half = width // 2
    for at in range(4):
        picked = jnp.concatenate(
            [tiles[tile, pl.ds(at, rows, stride=4), :] for tile in range(width // LANES)], axis=1
        ).astype(jnp.bfloat16)
        out_ref[2 * at] = picked[:, :half]
        out_ref[2 * at + 1] = picked[:, half:]


def attention_block(
    queries, keys, values, residual_in, out_proj, ln_gain, token_images, me_index, blocks, reach
):
    tok, width = queries.shape
    key_img = jnp.stack(
        [token_images(me_index + offset) for offset in range(-reach, reach + 1)]
    )[:, None, :]
    query_img = token_images(me_index)[:, None]
    vmem = pl.BlockSpec(memory_space=pltpu.VMEM)
    half = jnp.bfloat16
    return pl.pallas_call(
        functools.partial(attend_kernel, reach),
        out_shape=jax.ShapeDtypeStruct((8, tok // 4, width // 2), half),
        in_specs=[vmem] * 4 + [pl.BlockSpec(memory_space=pl.ANY)] + [vmem] * 3,
        out_specs=vmem,
        scratch_shapes=[
            pltpu.VMEM((width, width), half),
            pltpu.VMEM((reach, 2, tok, width), half),
            pltpu.VMEM((reach, 2, tok, width), half),
            pltpu.VMEM((HEADS, tok, 2 * LANES), half),
            pltpu.VMEM((HEADS, tok, 1), jnp.float32),
            pltpu.VMEM((HEADS, tok, 1), jnp.float32),
            pltpu.VMEM((HEADS, tok, 2 * LANES), jnp.float32),
            pltpu.VMEM((tok, tok), jnp.float32),
            pltpu.VMEM((tok, width), half),
            pltpu.VMEM((tok, width), jnp.float32),
            pltpu.VMEM((width // LANES, tok, LANES), jnp.float32),
            pltpu.SemaphoreType.DMA,
            pltpu.SemaphoreType.DMA((2, reach, 2)),
            pltpu.SemaphoreType.DMA((2, reach, 2)),
        ],
        compiler_params=pltpu.CompilerParams(
            collective_id=1, has_side_effects=True, vmem_limit_bytes=48 * 1024 * 1024
        ),
        cost_estimate=pl.CostEstimate(
            flops=4 * tok * tok * (2 * reach + 1) * width + 2 * tok * width * width,
            bytes_accessed=2 * width * width + 12 * tok * width,
            transcendentals=HEADS * tok * tok * (2 * reach + 1),
        ),
    )(queries, keys, values, residual_in, out_proj, ln_gain[None, :], query_img, key_img)


def on_device(
    queries, keys, values, residual_in, out_proj, ln_gain, merge_proj, out_gain, image_rows, owners
):
    blocks = lax.axis_size("blk")
    me_index = lax.axis_index("blk")
    tok, width = queries.shape
    row_count = tok // 4
    heads = HEADS
    hdim = width // heads
    reach = min(6, (blocks - 1) // 2)
    scale = 1.0 / hdim**0.5
    ends = jnp.cumsum(image_rows)

    def images_of(source, rows):
        found = jnp.sum((rows[:, None] >= ends[None, :]).astype(jnp.int32), axis=1)
        inside = jnp.logical_and(source >= 0, source < blocks)
        return jnp.where(inside, found, -1)

    def row_images(source):
        return images_of(source, source * row_count + jnp.arange(row_count, dtype=jnp.int32))

    def token_images(source):
        return images_of(source, source * row_count + jnp.arange(tok, dtype=jnp.int32) // 4)

    if blocks == 2 * CHIPS:
        feats_in = attention_block(
            queries, keys, values, residual_in, out_proj, ln_gain, token_images, me_index, blocks, reach
        )
        return merged_tail(
            feats_in, merge_proj, out_gain, image_rows, owners[:, 0], row_images(me_index), blocks
        )

    query_img = token_images(me_index)
    q_heads = queries.reshape(tok, heads, hdim)
    own_pair = jnp.stack([keys, values])

    def masked_scores(pair, key_img):
        k_heads = pair[0].reshape(-1, heads, hdim)
        scores = (
            jnp.einsum("qhd,khd->hqk", q_heads, k_heads, preferred_element_type=jnp.float32) * scale
        )
        return jnp.where(query_img[None, :, None] == key_img[None, None, :], scores, -jnp.inf)

    def weigh_values(weights, pair):
        v_heads = pair[1].reshape(-1, heads, hdim)
        return jnp.einsum(
            "hqk,khd->hqd",
            weights.astype(jnp.bfloat16),
            v_heads,
            preferred_element_type=jnp.float32,
        )

    def absorb(state, pair, key_img):

        def update(carry):
            running_max, running_sum, accum = carry
            scores = masked_scores(pair, key_img)
            new_max = jnp.maximum(running_max, jnp.max(scores, axis=2, keepdims=True))
            factor = jnp.exp(running_max - new_max)
            weights = jnp.exp(scores - new_max)
            new_sum = running_sum * factor + jnp.sum(weights, axis=2, keepdims=True)
            new_accum = accum * factor + weigh_values(weights, pair)
            return (new_max, new_sum, new_accum)

        live = jnp.logical_and(
            jnp.max(key_img) >= jnp.maximum(jnp.min(query_img), 0),
            jnp.min(jnp.where(key_img >= 0, key_img, 1 << 30)) <= jnp.max(query_img),
        )
        return lax.cond(live, update, lambda carry: carry, state)

    first_scores = masked_scores(own_pair, query_img)
    first_max = jnp.max(first_scores, axis=2, keepdims=True)
    first_weights = jnp.exp(first_scores - first_max)
    state = (
        first_max,
        jnp.sum(first_weights, axis=2, keepdims=True),
        weigh_values(first_weights, own_pair),
    )
    from_left = own_pair
    from_right = own_pair
    for step in range(1, reach + 1):
        from_left = passed_along(from_left, "blk", 1)
        state = absorb(state, from_left, token_images(me_index - step))
        from_right = passed_along(from_right, "blk", -1)
        state = absorb(state, from_right, token_images(me_index + step))
    heads_out = state[2] / state[1]
    attended = heads_out.transpose(1, 0, 2).reshape(tok, width).astype(jnp.bfloat16)
    stream = residual_in.astype(jnp.float32) + jnp.dot(
        attended, out_proj, preferred_element_type=jnp.float32
    )
    normed = layer_norm(stream, ln_gain).astype(jnp.bfloat16)
    merged = normed.reshape(row_count, 4 * width)
    feature_rows = lax.all_to_all(merged, "blk", split_axis=1, concat_axis=0, tiled=True)
    projected = lax.psum_scatter(
        jnp.dot(feature_rows, merge_proj, preferred_element_type=jnp.float32).astype(jnp.bfloat16),
        "blk",
        scatter_dimension=0,
        tiled=True,
    ).astype(jnp.float32)
    my_rows_img = row_images(me_index)
    nimg = image_rows.shape[0]
    member = (my_rows_img[:, None] == jnp.arange(nimg, dtype=jnp.int32)[None, :]).astype(
        jnp.float32
    )
    row_squares = jnp.sum(projected * projected, axis=1)
    image_sums = lax.psum(jnp.sum(member * row_squares[:, None], axis=0), "blk")
    out_width = projected.shape[1]
    image_mean = image_sums / (image_rows.astype(jnp.float32) * out_width)
    row_scale = jnp.sum(member * lax.rsqrt(image_mean + 1e-06)[None, :], axis=1)
    scaled = (projected * row_scale[:, None] * out_gain[None, :]).astype(jnp.bfloat16)
    capacity = max(2, 2 * row_count // blocks)
    owner = owners[:, 0]
    onehot = (owner[:, None] == jnp.arange(blocks, dtype=jnp.int32)[None, :]).astype(jnp.int32)
    rank = jnp.sum(jnp.cumsum(onehot, axis=0) * onehot, axis=1) - 1
    slot = owner * capacity + rank
    placement = (jnp.arange(blocks * capacity, dtype=jnp.int32)[:, None] == slot[None, :]).astype(
        jnp.bfloat16
    )
    outgoing = jnp.dot(placement, scaled, preferred_element_type=jnp.float32).astype(jnp.bfloat16)
    return lax.all_to_all(outgoing, "blk", split_axis=0, concat_axis=0, tiled=True)


def solution(mesh):
    in_specs = (
        P(("dp", "blk"), None),
        P(("dp", "blk"), None),
        P(("dp", "blk"), None),
        P(("dp", "blk"), None),
        P(),
        P(),
        P("blk", None),
        P(),
        P("dp"),
        P(("dp", "blk"), None),
    )
    out_specs = P(("dp", "blk"), None)
    return jax.shard_map(
        on_device, mesh=mesh, in_specs=in_specs, out_specs=out_specs, check_vma=False
    )
```

```python
import functools

import jax
import jax.numpy as jnp
from jax import lax
from jax.experimental import pallas as pl
from jax.experimental.pallas import tpu as pltpu
from jax.sharding import PartitionSpec as P

MESH = pl.DeviceIdType.MESH
CHIPS = 4
PARTS = 2
LANES = 128

HEADS = 16


def passed_along(value, axis, steps):
    count = lax.axis_size(axis)
    first, last = (max(0, -steps), min(count, count - steps))
    return lax.ppermute(value, axis, [(source, source + steps) for source in range(first, last)])


def layer_norm(stream, gain):
    mean = jnp.mean(stream, axis=1, keepdims=True)
    centred = stream - mean
    var = jnp.mean(centred * centred, axis=1, keepdims=True)
    return centred * lax.rsqrt(var + 1e-06) * gain[None, :]


def tail_kernel(
    feats_in,
    weight_hbm,
    member_ref,
    slot_member,
    place_ref,
    gain_ref,
    count_ref,
    out_ref,
    weight,
    feats,
    keep,
    give,
    taken,
    moving,
    from_left,
    from_right,
    packed,
    landed,
    slot_images,
    sums,
    weight_sem,
    feat_sems,
    slot_sems,
    pair_sems,
    line_sems,
    deliver_sems,
    sum_sems,
):
    blocks, rows, depth = feats_in.shape
    parts, width = keep.shape[0], keep.shape[3]
    cap = slot_member.shape[1]
    me = lax.axis_index("blk")
    chip, core = me // 2, lax.rem(me, 2)
    sibling = me + 1 - 2 * core

    def send(src, dst, sems, index, landing, target):
        return pltpu.make_async_remote_copy(
            src_ref=src,
            dst_ref=dst,
            send_sem=sems.at[(0,) + index],
            recv_sem=sems.at[(1,) + landing],
            device_id={"blk": target},
            device_id_type=MESH,
        )

    weight_copy = pltpu.make_async_copy(weight_hbm, weight, weight_sem)
    weight_copy.start()

    barrier = pltpu.get_barrier_semaphore()
    others = [lax.rem(me + step, blocks) for step in (4, 5, 3, 6, 2, 7, 1)]
    for other in others:
        pl.semaphore_signal(barrier, inc=1, device_id={"blk": other}, device_id_type=MESH)
    pl.semaphore_wait(barrier, blocks - 1)

    for other in others:
        send(feats_in.at[other], feats.at[me], feat_sems, (other,), (me,), other).start()
    feats[me] = feats_in[me]
    for other in others:
        send(slot_member.at[other], slot_images.at[me], slot_sems, (other,), (me,), other).start()
    slot_images[me] = slot_member[me]
    weight_copy.wait()

    def place_in_order(step):
        far = jnp.maximum(chip, CHIPS - 1 - chip)
        swapped = jnp.where(far == CHIPS - 1, step, 2 * CHIPS - 3 - step)
        low = jnp.where(step < 2, step, swapped)
        return jnp.where(chip >= 2, low, CHIPS - 1 - low)

    def wait_feats(source):
        @pl.when(source != me)
        def _():
            send(feats_in.at[source], feats.at[source], feat_sems, (source,), (source,), source).wait_recv()

    tile = 1024

    def multiply(part, first):
        def one(step, unused):
            to = place_in_order(step)
            if first:
                wait_feats(2 * to)
                wait_feats(2 * to + 1)
            lhs = jnp.concatenate([feats[2 * to + 1 - core], feats[2 * to + core]], axis=0)
            for at in range(0, width, tile):
                product = jnp.dot(
                    lhs,
                    weight[:, pl.ds(part * width + at, tile)],
                    preferred_element_type=jnp.float32,
                ).astype(jnp.bfloat16)
                give[part, to, :, pl.ds(at, tile)] = product[:rows]
                keep[part, to, :, pl.ds(at, tile)] = product[rows:]
            send(give.at[part, to], taken.at[part, to], pair_sems, (part, to), (part, to), sibling).start()
            return unused

        lax.fori_loop(0, CHIPS, one, 0)

    def pair_sum(part, to):
        send(give.at[part, to], taken.at[part, to], pair_sems, (part, to), (part, to), sibling).wait_recv()

    def pass_on(part, to, arrivals, direction, edge, way):
        pair_sum(part, to)

        @pl.when(edge)
        def _():
            moving[part, to] = (
                keep[part, to].astype(jnp.float32) + taken[part, to].astype(jnp.float32)
            ).astype(jnp.bfloat16)

        @pl.when(jnp.logical_not(edge))
        def _():
            line_copy(part, to, arrivals, way, direction).wait_recv()
            moving[part, to] = (
                keep[part, to].astype(jnp.float32)
                + taken[part, to].astype(jnp.float32)
                + arrivals[part, to].astype(jnp.float32)
            ).astype(jnp.bfloat16)

        line_copy(part, to, arrivals, way, direction).start()

    def line_copy(part, to, arrivals, way, direction):
        target = jnp.clip(me + direction, 0, blocks - 1)
        return pltpu.make_async_remote_copy(
            src_ref=moving.at[part, to],
            dst_ref=arrivals.at[part, to],
            send_sem=line_sems.at[0, part, to],
            recv_sem=line_sems.at[way, part, to],
            device_id={"blk": target},
            device_id_type=MESH,
        )

    def line_step(part, distance):
        @pl.when(chip + distance < CHIPS)
        def _():
            pass_on(part, chip + distance, from_left, 2, chip == 0, 1)

        @pl.when(chip - distance >= 0)
        def _():
            pass_on(part, chip - distance, from_right, -2, chip == CHIPS - 1, 2)

    def finish(part, squares):
        pair_sum(part, chip)

        @pl.when(chip > 0)
        def _():
            line_copy(part, chip, from_left, 1, 2).wait_recv()

        @pl.when(chip == 0)
        def _():
            from_left[part, chip] = jnp.zeros((rows, width), jnp.bfloat16)

        @pl.when(chip < CHIPS - 1)
        def _():
            line_copy(part, chip, from_right, 2, -2).wait_recv()

        @pl.when(chip == CHIPS - 1)
        def _():
            from_right[part, chip] = jnp.zeros((rows, width), jnp.bfloat16)

        step = 512
        for at in range(0, width, step):
            cols = pl.ds(at, step)
            total = (
                keep[part, chip, :, cols].astype(jnp.float32)
                + taken[part, chip, :, cols].astype(jnp.float32)
                + from_left[part, chip, :, cols].astype(jnp.float32)
                + from_right[part, chip, :, cols].astype(jnp.float32)
            )
            squares = squares + jnp.sum(total * total, axis=1, keepdims=True)
            slots = jnp.dot(
                place_ref[...], total.astype(jnp.bfloat16), preferred_element_type=jnp.float32
            ).astype(jnp.bfloat16)
            for owner in range(blocks):
                packed[part, owner, :, cols] = slots[owner * cap : (owner + 1) * cap]
        for other in others:
            send(packed.at[part, other], landed.at[part, me], deliver_sems, (part, other), (part, me), other).start()
        landed[part, me] = packed[part, me]
        return squares

    multiply(0, True)
    line_step(0, CHIPS - 1)
    for part in range(1, parts):
        multiply(part, False)
    for distance in range(CHIPS - 2, 0, -1):
        line_step(0, distance)
    squares = jnp.zeros((rows, 1), jnp.float32)
    for part in range(parts):
        if part + 1 < parts:
            for distance in range(CHIPS - 1, 0, -1):
                line_step(part + 1, distance)
        squares = finish(part, squares)

    mine = jnp.sum(member_ref[...] * squares, axis=0, keepdims=True)
    sums[me] = jnp.broadcast_to(mine, (8, LANES))
    for other in others:
        send(sums.at[me], sums.at[me], sum_sems, (other,), (me,), other).start()
    for other in others:
        send(sums.at[me], sums.at[other], sum_sems, (other,), (other,), other).wait_recv()
    total = sums[0]
    for source in range(1, blocks):
        total = total + sums[source]
    inverse = lax.rsqrt(total / count_ref[...] + 1e-06)[0:1]

    for step in range(blocks):
        source = me if step == 0 else others[blocks - 1 - step]
        if step:
            send(slot_member.at[source], slot_images.at[source], slot_sems, (source,), (source,), source).wait_recv()
        row_scale = jnp.sum(slot_images[source] * inverse, axis=1, keepdims=True)
        lines = pl.ds(pl.multiple_of(source * cap, cap), cap)
        for part in range(parts):
            if step:
                send(
                    packed.at[part, source], landed.at[part, source], deliver_sems, (part, source), (part, source), source
                ).wait_recv()
            out_ref[lines, pl.ds(part * width, width)] = (
                landed[part, source].astype(jnp.float32)
                * row_scale
                * gain_ref[:, pl.ds(part * width, width)]
            ).astype(jnp.bfloat16)

    for other in others:
        send(feats_in.at[other], feats.at[me], feat_sems, (other,), (me,), other).wait_send()
        send(slot_member.at[other], slot_images.at[me], slot_sems, (other,), (me,), other).wait_send()
        send(sums.at[me], sums.at[me], sum_sems, (other,), (me,), other).wait_send()
        for part in range(parts):
            send(packed.at[part, other], landed.at[part, me], deliver_sems, (part, other), (part, me), other).wait_send()
    for part in range(parts):
        for to in range(CHIPS):
            send(give.at[part, to], taken.at[part, to], pair_sems, (part, to), (part, to), sibling).wait_send()

            @pl.when(chip < to)
            def _():
                line_copy(part, to, from_left, 1, 2).wait_send()

            @pl.when(chip > to)
            def _():
                line_copy(part, to, from_right, 2, -2).wait_send()


def merged_tail(feats_in, merge_proj, out_gain, image_rows, owner, my_rows_img, blocks):
    rows = feats_in.shape[1]
    depth, out_width = merge_proj.shape
    nimg = image_rows.shape[0]
    cap = max(2, 2 * rows // blocks)
    width = out_width // PARTS
    lanes = jnp.arange(LANES, dtype=jnp.int32)
    member = (my_rows_img[:, None] == lanes[None, :]).astype(jnp.float32)
    onehot = (owner[:, None] == jnp.arange(blocks, dtype=jnp.int32)[None, :]).astype(jnp.int32)
    rank = jnp.sum(jnp.cumsum(onehot, axis=0) * onehot, axis=1) - 1
    slot = owner * cap + rank
    filled = jnp.arange(blocks * cap, dtype=jnp.int32)[:, None] == slot[None, :]
    place = filled.astype(jnp.bfloat16)
    slot_img = jnp.sum(jnp.where(filled, my_rows_img[None, :] + 1, 0), axis=1) - 1
    slot_member = (slot_img[:, None] == lanes[None, :]).astype(jnp.float32)
    slot_member = slot_member.reshape(blocks, cap, LANES)
    counts = jnp.ones((LANES,), jnp.float32).at[:nimg].set(
        image_rows.astype(jnp.float32) * out_width
    )
    counts = jnp.broadcast_to(counts[None, :], (8, LANES))
    vmem = pl.BlockSpec(memory_space=pltpu.VMEM)
    tiles = (PARTS, CHIPS, rows, width)
    half = jnp.bfloat16
    return pl.pallas_call(
        tail_kernel,
        out_shape=jax.ShapeDtypeStruct((blocks * cap, out_width), half),
        in_specs=[vmem, pl.BlockSpec(memory_space=pl.ANY)] + [vmem] * 5,
        out_specs=vmem,
        scratch_shapes=[
            pltpu.VMEM((depth, out_width), half),
            pltpu.VMEM((blocks, rows, depth), half),
            pltpu.VMEM(tiles, half),
            pltpu.VMEM(tiles, half),
            pltpu.VMEM(tiles, half),
            pltpu.VMEM(tiles, half),
            pltpu.VMEM(tiles, half),
            pltpu.VMEM(tiles, half),
            pltpu.VMEM((PARTS, blocks, cap, width), half),
            pltpu.VMEM((PARTS, blocks, cap, width), half),
            pltpu.VMEM((blocks, cap, LANES), jnp.float32),
            pltpu.VMEM((blocks, 8, LANES), jnp.float32),
            pltpu.SemaphoreType.DMA,
            pltpu.SemaphoreType.DMA((2, blocks)),
            pltpu.SemaphoreType.DMA((2, blocks)),
            pltpu.SemaphoreType.DMA((2, PARTS, CHIPS)),
            pltpu.SemaphoreType.DMA((3, PARTS, CHIPS)),
            pltpu.SemaphoreType.DMA((2, PARTS, blocks)),
            pltpu.SemaphoreType.DMA((2, blocks)),
        ],
        compiler_params=pltpu.CompilerParams(
            collective_id=0, has_side_effects=True, vmem_limit_bytes=58 * 1024 * 1024
        ),
        cost_estimate=pl.CostEstimate(
            flops=2 * rows * blocks * depth * out_width,
            bytes_accessed=2 * depth * out_width,
            transcendentals=0,
        ),
    )(feats_in, merge_proj, member, slot_member, place, out_gain[None, :], counts)


def attend_kernel(
    reach,
    q_ref,
    k_ref,
    v_ref,
    res_ref,
    proj_hbm,
    gain_ref,
    query_img,
    key_img,
    out_ref,
    proj,
    from_left,
    from_right,
    q_heads,
    tops,
    totals,
    accum,
    bias,
    attended,
    stream,
    tiles,
    proj_sem,
    right_sems,
    left_sems,
):
    tok, width = q_ref.shape
    hdim = width // HEADS
    blocks = lax.axis_size("blk")
    me = lax.axis_index("blk")
    scale = 1.4426950408889634 / hdim**0.5

    proj_copy = pltpu.make_async_copy(proj_hbm, proj, proj_sem)
    proj_copy.start()

    barrier = pltpu.get_barrier_semaphore()

    @pl.when(me > 0)
    def _():
        pl.semaphore_signal(barrier, inc=1, device_id={"blk": me - 1}, device_id_type=MESH)

    @pl.when(me < blocks - 1)
    def _():
        pl.semaphore_signal(barrier, inc=1, device_id={"blk": me + 1}, device_id_type=MESH)

    at_end = jnp.logical_or(me == 0, me == blocks - 1)

    @pl.when(at_end)
    def _():
        pl.semaphore_wait(barrier, 1)

    @pl.when(jnp.logical_not(at_end))
    def _():
        pl.semaphore_wait(barrier, 2)

    def pair_copies(step, buffers, sems, direction):
        target = jnp.clip(me + direction, 0, blocks - 1)
        found = []
        for which, own in ((0, k_ref), (1, v_ref)):
            found.append(
                pltpu.make_async_remote_copy(
                    src_ref=own if step == 1 else buffers.at[step - 2, which],
                    dst_ref=buffers.at[step - 1, which],
                    send_sem=sems.at[0, step - 1, which],
                    recv_sem=sems.at[1, step - 1, which],
                    device_id={"blk": target},
                    device_id_type=MESH,
                )
            )
        return found

    ways = ((from_left, right_sems, 1), (from_right, left_sems, -1))

    def sends(step, direction):
        if direction > 0:
            return jnp.logical_and(me + 1 < blocks, me - step + 1 >= 0)
        return jnp.logical_and(me >= 1, me + step - 1 < blocks)

    def comes(step, direction):
        return me - step >= 0 if direction > 0 else me + step < blocks

    def start(step, way):
        @pl.when(sends(step, way[2]))
        def _():
            for copy in pair_copies(step, *way):
                copy.start()

    def wait_send(step, way):
        @pl.when(sends(step, way[2]))
        def _():
            for copy in pair_copies(step, *way):
                copy.wait_send()

    def wait_recv(step, way):
        @pl.when(comes(step, way[2]))
        def _():
            for copy in pair_copies(step, *way):
                copy.wait_recv()

    def window(head):
        return min(head * hdim // LANES, width // LANES - 2) * LANES

    def of_head(head):
        column = window(head) + lax.broadcasted_iota(jnp.int32, (tok, 2 * LANES), 1)
        return jnp.logical_and(column >= head * hdim, column < (head + 1) * hdim)

    def attend(k_at, v_at, images, first):
        bias[...] = jnp.where(query_img[...] == images, 0.0, -jnp.inf)
        for head in range(HEADS):
            cols = pl.ds(window(head), 2 * LANES)
            scores = (
                lax.dot_general(
                    k_at[:, cols],
                    q_heads[head],
                    (((1,), (1,)), ((), ())),
                    preferred_element_type=jnp.float32,
                )
                * scale
                + bias[...]
            )
            top = jnp.max(scores, axis=0, keepdims=True)
            if not first:
                before = tops[head]
                top = jnp.maximum(before, top)
                factor = jnp.exp2(before - top)
            weights = jnp.exp2(scores - top)
            total = jnp.sum(weights, axis=0, keepdims=True)
            found = lax.dot_general(
                v_at[:, cols],
                weights.astype(jnp.bfloat16),
                (((0,), (0,)), ((), ())),
                preferred_element_type=jnp.float32,
            )
            begin = head * hdim - window(head)
            found = found[begin : begin + hdim]
            if not first:
                total = totals[head] * factor + total
                found = accum[head] * factor + found
            tops[head] = top
            totals[head] = total
            accum[head] = found

    for way in ways:
        start(1, way)
    for head in range(HEADS):
        cols = pl.ds(window(head), 2 * LANES)
        q_heads[head] = jnp.where(of_head(head), q_ref[:, cols], jnp.zeros((), jnp.bfloat16))
    attend(k_ref, v_ref, key_img[reach], True)
    for step in range(1, reach + 1):
        for way in ways:
            wait_recv(step, way)
            wait_send(step, way)
            if step < reach:
                start(step + 1, way)
        for buffers, _, direction in ways:

            @pl.when(comes(step, direction))
            def _():
                attend(
                    buffers.at[step - 1, 0],
                    buffers.at[step - 1, 1],
                    key_img[reach - direction * step],
                    False,
                )

    for head in range(0, HEADS, 2):
        found = jnp.concatenate(
            [accum[head] / totals[head], accum[head + 1] / totals[head + 1]], axis=0
        )
        attended[pl.ds(head * hdim, 2 * hdim), :] = found.astype(jnp.bfloat16)

    proj_copy.wait()
    tile = 512
    for at in range(0, width, tile):
        cols = pl.ds(at, min(tile, width - at))
        stream[:, cols] = res_ref[:, cols].astype(jnp.float32) + lax.dot_general(
            attended[...],
            proj[:, cols],
            (((0,), (0,)), ((), ())),
            preferred_element_type=jnp.float32,
        )
    rows = tok // 4
    for at in range(0, tok, rows):
        lines = pl.ds(at, rows)
        normed = layer_norm(stream[lines, :], gain_ref[0])
        for tile in range(width // LANES):
            tiles[tile, lines, :] = normed[:, tile * LANES : (tile + 1) * LANES]
    half = width // 2
    for at in range(4):
        picked = jnp.concatenate(
            [tiles[tile, pl.ds(at, rows, stride=4), :] for tile in range(width // LANES)], axis=1
        ).astype(jnp.bfloat16)
        out_ref[2 * at] = picked[:, :half]
        out_ref[2 * at + 1] = picked[:, half:]


def attention_block(
    queries, keys, values, residual_in, out_proj, ln_gain, token_images, me_index, blocks, reach
):
    tok, width = queries.shape
    key_img = jnp.stack(
        [token_images(me_index + offset) for offset in range(-reach, reach + 1)]
    )[:, :, None]
    query_img = token_images(me_index)[None, :]
    vmem = pl.BlockSpec(memory_space=pltpu.VMEM)
    half = jnp.bfloat16
    return pl.pallas_call(
        functools.partial(attend_kernel, reach),
        out_shape=jax.ShapeDtypeStruct((8, tok // 4, width // 2), half),
        in_specs=[vmem] * 4 + [pl.BlockSpec(memory_space=pl.ANY)] + [vmem] * 3,
        out_specs=vmem,
        scratch_shapes=[
            pltpu.VMEM((width, width), half),
            pltpu.VMEM((reach, 2, tok, width), half),
            pltpu.VMEM((reach, 2, tok, width), half),
            pltpu.VMEM((HEADS, tok, 2 * LANES), half),
            pltpu.VMEM((HEADS, 1, tok), jnp.float32),
            pltpu.VMEM((HEADS, 1, tok), jnp.float32),
            pltpu.VMEM((HEADS, width // HEADS, tok), jnp.float32),
            pltpu.VMEM((tok, tok), jnp.float32),
            pltpu.VMEM((width, tok), half),
            pltpu.VMEM((tok, width), jnp.float32),
            pltpu.VMEM((width // LANES, tok, LANES), jnp.float32),
            pltpu.SemaphoreType.DMA,
            pltpu.SemaphoreType.DMA((2, reach, 2)),
            pltpu.SemaphoreType.DMA((2, reach, 2)),
        ],
        compiler_params=pltpu.CompilerParams(
            collective_id=1, has_side_effects=True, vmem_limit_bytes=48 * 1024 * 1024
        ),
        cost_estimate=pl.CostEstimate(
            flops=4 * tok * tok * (2 * reach + 1) * width + 2 * tok * width * width,
            bytes_accessed=2 * width * width + 12 * tok * width,
            transcendentals=HEADS * tok * tok * (2 * reach + 1),
        ),
    )(queries, keys, values, residual_in, out_proj, ln_gain[None, :], query_img, key_img)


def on_device(
    queries, keys, values, residual_in, out_proj, ln_gain, merge_proj, out_gain, image_rows, owners
):
    blocks = lax.axis_size("blk")
    me_index = lax.axis_index("blk")
    tok, width = queries.shape
    row_count = tok // 4
    heads = HEADS
    hdim = width // heads
    reach = min(6, (blocks - 1) // 2)
    scale = 1.0 / hdim**0.5
    ends = jnp.cumsum(image_rows)

    def images_of(source, rows):
        found = jnp.sum((rows[:, None] >= ends[None, :]).astype(jnp.int32), axis=1)
        inside = jnp.logical_and(source >= 0, source < blocks)
        return jnp.where(inside, found, -1)

    def row_images(source):
        return images_of(source, source * row_count + jnp.arange(row_count, dtype=jnp.int32))

    def token_images(source):
        return images_of(source, source * row_count + jnp.arange(tok, dtype=jnp.int32) // 4)

    if blocks == 2 * CHIPS:
        feats_in = attention_block(
            queries, keys, values, residual_in, out_proj, ln_gain, token_images, me_index, blocks, reach
        )
        return merged_tail(
            feats_in, merge_proj, out_gain, image_rows, owners[:, 0], row_images(me_index), blocks
        )

    query_img = token_images(me_index)
    q_heads = queries.reshape(tok, heads, hdim)
    own_pair = jnp.stack([keys, values])

    def masked_scores(pair, key_img):
        k_heads = pair[0].reshape(-1, heads, hdim)
        scores = (
            jnp.einsum("qhd,khd->hqk", q_heads, k_heads, preferred_element_type=jnp.float32) * scale
        )
        return jnp.where(query_img[None, :, None] == key_img[None, None, :], scores, -jnp.inf)

    def weigh_values(weights, pair):
        v_heads = pair[1].reshape(-1, heads, hdim)
        return jnp.einsum(
            "hqk,khd->hqd",
            weights.astype(jnp.bfloat16),
            v_heads,
            preferred_element_type=jnp.float32,
        )

    def absorb(state, pair, key_img):

        def update(carry):
            running_max, running_sum, accum = carry
            scores = masked_scores(pair, key_img)
            new_max = jnp.maximum(running_max, jnp.max(scores, axis=2, keepdims=True))
            factor = jnp.exp(running_max - new_max)
            weights = jnp.exp(scores - new_max)
            new_sum = running_sum * factor + jnp.sum(weights, axis=2, keepdims=True)
            new_accum = accum * factor + weigh_values(weights, pair)
            return (new_max, new_sum, new_accum)

        live = jnp.logical_and(
            jnp.max(key_img) >= jnp.maximum(jnp.min(query_img), 0),
            jnp.min(jnp.where(key_img >= 0, key_img, 1 << 30)) <= jnp.max(query_img),
        )
        return lax.cond(live, update, lambda carry: carry, state)

    first_scores = masked_scores(own_pair, query_img)
    first_max = jnp.max(first_scores, axis=2, keepdims=True)
    first_weights = jnp.exp(first_scores - first_max)
    state = (
        first_max,
        jnp.sum(first_weights, axis=2, keepdims=True),
        weigh_values(first_weights, own_pair),
    )
    from_left = own_pair
    from_right = own_pair
    for step in range(1, reach + 1):
        from_left = passed_along(from_left, "blk", 1)
        state = absorb(state, from_left, token_images(me_index - step))
        from_right = passed_along(from_right, "blk", -1)
        state = absorb(state, from_right, token_images(me_index + step))
    heads_out = state[2] / state[1]
    attended = heads_out.transpose(1, 0, 2).reshape(tok, width).astype(jnp.bfloat16)
    stream = residual_in.astype(jnp.float32) + jnp.dot(
        attended, out_proj, preferred_element_type=jnp.float32
    )
    normed = layer_norm(stream, ln_gain).astype(jnp.bfloat16)
    merged = normed.reshape(row_count, 4 * width)
    feature_rows = lax.all_to_all(merged, "blk", split_axis=1, concat_axis=0, tiled=True)
    projected = lax.psum_scatter(
        jnp.dot(feature_rows, merge_proj, preferred_element_type=jnp.float32).astype(jnp.bfloat16),
        "blk",
        scatter_dimension=0,
        tiled=True,
    ).astype(jnp.float32)
    my_rows_img = row_images(me_index)
    nimg = image_rows.shape[0]
    member = (my_rows_img[:, None] == jnp.arange(nimg, dtype=jnp.int32)[None, :]).astype(
        jnp.float32
    )
    row_squares = jnp.sum(projected * projected, axis=1)
    image_sums = lax.psum(jnp.sum(member * row_squares[:, None], axis=0), "blk")
    out_width = projected.shape[1]
    image_mean = image_sums / (image_rows.astype(jnp.float32) * out_width)
    row_scale = jnp.sum(member * lax.rsqrt(image_mean + 1e-06)[None, :], axis=1)
    scaled = (projected * row_scale[:, None] * out_gain[None, :]).astype(jnp.bfloat16)
    capacity = max(2, 2 * row_count // blocks)
    owner = owners[:, 0]
    onehot = (owner[:, None] == jnp.arange(blocks, dtype=jnp.int32)[None, :]).astype(jnp.int32)
    rank = jnp.sum(jnp.cumsum(onehot, axis=0) * onehot, axis=1) - 1
    slot = owner * capacity + rank
    placement = (jnp.arange(blocks * capacity, dtype=jnp.int32)[:, None] == slot[None, :]).astype(
        jnp.bfloat16
    )
    outgoing = jnp.dot(placement, scaled, preferred_element_type=jnp.float32).astype(jnp.bfloat16)
    return lax.all_to_all(outgoing, "blk", split_axis=0, concat_axis=0, tiled=True)


def solution(mesh):
    in_specs = (
        P(("dp", "blk"), None),
        P(("dp", "blk"), None),
        P(("dp", "blk"), None),
        P(("dp", "blk"), None),
        P(),
        P(),
        P("blk", None),
        P(),
        P("dp"),
        P(("dp", "blk"), None),
    )
    out_specs = P(("dp", "blk"), None)
    return jax.shard_map(
        on_device, mesh=mesh, in_specs=in_specs, out_specs=out_specs, check_vma=False
    )
```
